32 devices in a mesh: grp: 2 (over x), grid: 16 (over z, y, core).
Axes of the slice: x: 2, y: 2, z: 4, core: 2. Of those that a mesh axis runs over, the one named last changes fastest.
Arguments:
- valence: bfloat16 [32768, 48], P(('grp', 'grid')), parts along dimension 0, may hold values from -24 to 24
- conduction: bfloat16 [32768, 512], P(('grp', 'grid')), parts along dimension 0, may hold values from -6 to 6
- potentials: bfloat16 [32768, 64], P(('grp', 'grid')), parts along dimension 0, may hold values from -6 to 6
- eigenpotentials: bfloat16 [32768, 1024], P(('grp', 'grid')), parts along dimension 0, may hold values from -0.1875 to 0.1875
- valence_energy: float32 [96], P('grp'), parts along dimension 0, may hold values from -6 to -1
- conduction_energy: float32 [1024], P('grp'), parts along dimension 0, may hold values from 0.5 to 20
Outputs:
- projected: float32 [2048, 64], P(('grp', 'grid')), parts along dimension 0
- complementary: float32 [32768, 64], P(('grp', 'grid')), parts along dimension 0
The draws below stay inside these ranges and needn't reach their ends.
There are 2 independent parts, one for each index of `grp`. The reference program is written for one: setup_inputs(seed, part) draws one part's arguments, and reference() takes and returns one part's arrays. A program takes and returns all parts, laid end to end along the dimension named above; each array names one. Nothing has to cross between parts.
All inputs are finite; a program needn't handle non-finite values.
Results may differ from the reference program's by a relative error of at most 0.0042.
Values may be sent and summed in bfloat16 or wider, within the bound.
A program may use at most 64 MiB of HBM per device.

```python
import math
import jax
import jax.numpy as jnp
from jax import lax

NV = 48
NC = 512
NP = 64
NE = 1024
POINTS = 16384


def draw_valence(key, part):
    key_list = jax.random.split(key, 3)
    position = jnp.arange(POINTS, dtype=jnp.float32) / (POINTS - 1)
    envelope = jnp.sqrt(1.0 + 2.0 * position)
    values = jnp.clip(jax.random.normal(key_list[0], (POINTS, NV), jnp.float32), -4.0, 4.0)
    spread = 10.0 ** jax.random.uniform(key_list[2], (POINTS, 1), jnp.float32, -0.5, 0.5)
    return jnp.clip(values * envelope[:, None] * spread, -24.0, 24.0).astype(jnp.bfloat16)


def draw_eigenpotentials(key, part):
    key_list = jax.random.split(key, 2)
    column = jnp.arange(NE, dtype=jnp.float32) / (NE - 1)
    spread = 10.0 ** jax.random.uniform(key_list[1], (1, NE), jnp.float32, -0.5, 0.5)
    envelope = jnp.sqrt(1.0 + 2.0 * column)
    values = jnp.clip(jax.random.normal(key_list[0], (POINTS, NE), jnp.float32), -4.0, 4.0)
    factor = POINTS ** (-0.5)
    return jnp.clip(values * envelope[None, :] * spread * factor, -24.0 * factor, 24.0 * factor).astype(jnp.bfloat16)


def steps_of(rng, extent, shards, low, largest):
    level = 1.0
    for dim, parts in shards:
        steps = jax.random.uniform(jax.random.fold_in(jax.random.fold_in(rng, 6), dim), (parts,), jnp.float32, low / len(shards), largest / len(shards))
        level = level * jnp.repeat(jnp.exp(steps), extent[dim] // parts).reshape((-1,) + (1,) * (len(extent) - 1 - dim))
    return level


def noise(own_key, shape, width, reach, cuts=(), held_as=jnp.bfloat16):
    level = steps_of(own_key, shape, cuts, -0.22, 0.18) if cuts else 1.0
    result = jax.random.normal(own_key, shape, jnp.float32) * width * level
    return jnp.minimum(jnp.maximum(result, -reach), reach).astype(held_as)


def setup_inputs(seed: int = 0, part: int = 0) -> dict:
    arg_keys = jax.random.split(jax.random.key(seed), 7)
    part_keys = jax.random.split(jax.random.fold_in(arg_keys[6], part), 7)
    return {
        "valence": draw_valence(jax.random.fold_in(jax.random.fold_in(arg_keys[6], part), 71), part),
        "conduction": noise(part_keys[1], (POINTS, NC), 1.0, 6.0, ((0, 16),)),
        "potentials": noise(part_keys[2], (POINTS, NP), 1.0, 6.0, ((0, 16),)),
        "eigenpotentials": draw_eigenpotentials(jax.random.fold_in(jax.random.fold_in(arg_keys[6], part), 71), part),
        "valence_energy": jnp.clip(jax.random.uniform(part_keys[4], (NV,), jnp.float32, -6.0, -1.0), -6.0, -1.0),
        "conduction_energy": jnp.clip(jnp.exp(jax.random.uniform(part_keys[5], (NC,), jnp.float32, math.log(0.5), math.log(20.0))), 0.5, 20.0),
    }


def pair_products(val_block, pot_block):
    joined = pot_block.astype(jnp.float32)[:, :, None] * val_block.astype(jnp.float32)[:, None, :]
    return joined.reshape(val_block.shape[0], -1).astype(jnp.bfloat16)

def reference(valence, conduction, potentials, eigenpotentials, valence_energy, conduction_energy):
    points_total = valence.shape[0]
    valence_count = valence.shape[1]
    conduction_count = conduction.shape[1]
    potential_count = potentials.shape[1]
    block_size = min(4096, points_total)
    block_count = points_total // block_size
    val_blocks = valence.reshape(block_count, block_size, valence_count)
    cond_blocks = conduction.reshape(block_count, block_size, conduction_count)
    pot_blocks = potentials.reshape(block_count, block_size, potential_count)

    def add_block(carried, blocks_in):
        val_block, cond_block, pot_block = blocks_in
        paired = pair_products(val_block, pot_block)
        return (carried + lax.dot_general(cond_block, paired, (((0,), (0,)), ((), ())), preferred_element_type=jnp.float32), None)
    initial = jnp.zeros((conduction_count, potential_count * valence_count), jnp.float32)
    coefficients, _ = lax.scan(add_block, initial, (val_blocks, cond_blocks, pot_blocks))
    denominators = valence_energy[None, :] - conduction_energy[:, None]
    scaled = (coefficients.reshape(conduction_count, potential_count, valence_count) * (4.0 / points_total) / denominators[:, None, :]).reshape(conduction_count, potential_count * valence_count).astype(jnp.bfloat16)

    def respond(blocks_in):
        val_block, cond_block = blocks_in
        combined = jnp.dot(cond_block, scaled, preferred_element_type=jnp.float32)
        return lax.optimization_barrier(jnp.sum(combined.reshape(block_size, potential_count, valence_count) * val_block.astype(jnp.float32)[:, None, :], axis=2))
    response = lax.map(respond, (val_blocks, cond_blocks)).reshape(points_total, potential_count)
    response_low = response.astype(jnp.bfloat16)
    intersection = lax.dot_general(eigenpotentials, response_low, (((0,), (0,)), ((), ())), preferred_element_type=jnp.float32)
    projected = intersection / jnp.sqrt(lax.optimization_barrier(jnp.mean(intersection * intersection, axis=0)) + 1e-06)
    intersection_low = intersection.astype(jnp.bfloat16)
    remainder = response - jnp.dot(eigenpotentials, intersection_low, preferred_element_type=jnp.float32)
    complementary = remainder / jnp.sqrt(lax.optimization_barrier(jnp.mean(remainder * remainder, axis=0)) + 1e-06)
    return (projected, complementary)
```

```python
import functools

import jax
import jax.numpy as jnp
from jax import lax
from jax.experimental import pallas as pl
from jax.experimental.pallas import tpu as pltpu
from jax.sharding import PartitionSpec as P

MESH = pl.DeviceIdType.MESH
VMEM_BYTES = 56 * 1024 * 1024


def contract_rows(left, right):
    return lax.dot_general(
        left, right, (((0,), (0,)), ((), ())), preferred_element_type=jnp.float32
    )


def bit_of(me, bit):
    return lax.rem(lax.div(me, 1 << bit), 2)


def partner_of(me, bit):
    return me + (1 - 2 * bit_of(me, bit)) * (1 << bit)


def aligned(row, step):
    return pl.multiple_of(row, step)


def reversed_bits(value, bits):
    return sum(((value >> b) & 1) << (bits - 1 - b) for b in range(bits))


def couple_kernel(n, orders, part_ref, weight_ref, out_ref, acc, sent, got, send_sem, recv_sem):
    levels = n.bit_length() - 1
    me = lax.axis_index("grid")
    rows, columns = part_ref.shape
    unit = weight_ref.shape[0]
    block = rows // n
    width = columns // len(orders)

    barrier = pltpu.get_barrier_semaphore()
    for bit in range(levels):
        pl.semaphore_signal(
            barrier, inc=1, device_id={"grid": partner_of(me, bit)}, device_id_type=MESH
        )
    pl.semaphore_wait(barrier, levels)

    slots = [rows - (rows >> s) for s in range(levels)]
    bases = [[0] for _ in orders]
    copies = [[] for _ in orders]

    for s in range(levels + 1):
        for q, order in enumerate(orders):
            cols = pl.ds(q * width, width)
            base = bases[q][s]
            source = part_ref if s <= 1 else acc
            if s > 0:
                copies[q][s - 1].wait_recv()

            def term(row, offset, s=s, source=source, cols=cols):
                value = source[pl.ds(aligned(row + offset, unit), unit), cols]
                if s > 0:
                    value = value + got[
                        pl.ds(aligned(slots[s - 1] + offset, unit), unit), cols
                    ].astype(jnp.float32)
                return value

            if s == levels:
                def finish(i, _, term=term, base=base, cols=cols):
                    scaled = term(base * block, i * unit) * weight_ref[:, cols]
                    out_ref[pl.ds(aligned(base * block + i * unit, unit), unit), cols] = (
                        scaled.astype(jnp.bfloat16)
                    )
                    return 0

                lax.fori_loop(0, block // unit, finish, 0)
                continue
            half = n >> (s + 1)
            bit = bit_of(me, order[s])
            leave, keep = (1 - bit) * half * block, bit * half * block

            def pack(i, _, term=term, base=base, leave=leave, s=s, cols=cols):
                sent[pl.ds(aligned(slots[s] + i * unit, unit), unit), cols] = term(
                    base * block, leave + i * unit
                ).astype(jnp.bfloat16)
                return 0

            lax.fori_loop(0, half * block // unit, pack, 0)
            copy = pltpu.make_async_remote_copy(
                src_ref=sent.at[pl.ds(slots[s], half * block), cols],
                dst_ref=got.at[pl.ds(slots[s], half * block), cols],
                send_sem=send_sem.at[q, s],
                recv_sem=recv_sem.at[q, s],
                device_id={"grid": partner_of(me, order[s])},
                device_id_type=MESH,
            )
            copy.start()
            copies[q].append(copy)
            if s > 0:
                def add(i, _, term=term, base=base, keep=keep, cols=cols):
                    acc[pl.ds(aligned(base * block + keep + i * unit, unit), unit), cols] = term(
                        base * block, keep + i * unit
                    )
                    return 0

                lax.fori_loop(0, half * block // unit, add, 0)
            bases[q].append(base + bit * half)

    for s in reversed(range(levels)):
        for q, order in enumerate(orders):
            if s < levels - 1:
                copies[q][-1].wait_recv()
            size = (n >> (s + 1)) * block
            view = out_ref.at[
                pl.ds(aligned(bases[q][s + 1] * block, unit), size), pl.ds(q * width, width)
            ]
            copy = pltpu.make_async_remote_copy(
                src_ref=view,
                dst_ref=view,
                send_sem=send_sem.at[q, 2 * levels - 1 - s],
                recv_sem=recv_sem.at[q, 2 * levels - 1 - s],
                device_id={"grid": partner_of(me, order[s])},
                device_id_type=MESH,
            )
            copy.start()
            copies[q].append(copy)
    for q in range(len(orders)):
        copies[q][-1].wait_recv()
        for copy in copies[q]:
            copy.wait_send()


def project_kernel(
    n, eigen_ref, response_ref, projected_ref, complementary_ref,
    acc, got, gathered, low, sums, send_sem, recv_sem, sum_send, sum_recv,
):
    levels = n.bit_length() - 1
    me = lax.axis_index("grid")
    points, eigens = eigen_ref.shape
    block = eigens // n

    barrier = pltpu.get_barrier_semaphore()
    for offset in range(1, n):
        pl.semaphore_signal(
            barrier, inc=1, device_id={"grid": lax.rem(me + offset, n)}, device_id_type=MESH
        )

    response_low = response_ref[...].astype(jnp.bfloat16)
    strip = min(256, eigens)
    for start in range(0, eigens, strip):
        strip_sum = contract_rows(eigen_ref[:, start:start + strip], response_low)
        for b in range(strip // block):
            place = reversed_bits(start // block + b, levels) * block
            acc[place:place + block, :] = strip_sum[b * block:(b + 1) * block, :]
    pl.semaphore_wait(barrier, n - 1)

    slots = [eigens - (eigens >> s) for s in range(levels)]
    bases = [0]
    copies = []
    for s in range(levels):
        half = n >> (s + 1)
        bit = bit_of(me, s)
        leave = (bases[s] + (1 - bit) * half) * block
        keep = (bases[s] + bit * half) * block
        copy = pltpu.make_async_remote_copy(
            src_ref=acc.at[pl.ds(aligned(leave, block), half * block)],
            dst_ref=got.at[pl.ds(slots[s], half * block)],
            send_sem=send_sem.at[s],
            recv_sem=recv_sem.at[s],
            device_id={"grid": partner_of(me, s)},
            device_id_type=MESH,
        )
        copy.start()
        copies.append(copy)
        copy.wait_recv()
        kept = pl.ds(aligned(keep, block), half * block)
        acc[kept, :] = acc[kept, :] + got[pl.ds(slots[s], half * block), :]
        bases.append(bases[s] + bit * half)

    own = pl.ds(aligned(bases[levels] * block, block), block)
    mine = acc[own, :]
    gathered[own, :] = mine.astype(jnp.bfloat16)
    for s in reversed(range(levels)):
        view = gathered.at[pl.ds(aligned(bases[s + 1] * block, block), (n >> (s + 1)) * block)]
        copy = pltpu.make_async_remote_copy(
            src_ref=view,
            dst_ref=view,
            send_sem=send_sem.at[2 * levels - 1 - s],
            recv_sem=recv_sem.at[2 * levels - 1 - s],
            device_id={"grid": partner_of(me, s)},
            device_id_type=MESH,
        )
        copy.start()
        copies.append(copy)
        copy.wait_recv()
    for b in range(n):
        place = reversed_bits(b, levels) * block
        low[b * block:(b + 1) * block, :] = gathered[place:place + block, :]

    intersection_low = low[...]
    remainder = response_ref[...] - jnp.dot(
        eigen_ref[...], intersection_low, preferred_element_type=jnp.float32
    )
    sums[me] = jnp.broadcast_to(
        jnp.sum(remainder * remainder, axis=0, keepdims=True), sums.shape[1:]
    )
    for offset in range(1, n):
        copy = pltpu.make_async_remote_copy(
            src_ref=sums.at[me],
            dst_ref=sums.at[me],
            send_sem=sum_send.at[offset],
            recv_sem=sum_recv.at[offset],
            device_id={"grid": lax.rem(me + offset, n)},
            device_id_type=MESH,
        )
        copy.start()
        copies.append(copy)
    complementary_ref[...] = remainder
    wide = intersection_low.astype(jnp.float32)
    squares = jnp.sum(wide * wide, axis=0, keepdims=True)
    projected_ref[...] = mine / jnp.sqrt(squares / eigens + 1e-06)
    for offset in range(1, n):
        other = lax.rem(me + n - offset, n)
        pltpu.make_async_remote_copy(
            src_ref=sums.at[other],
            dst_ref=sums.at[other],
            send_sem=sum_send.at[offset],
            recv_sem=sum_recv.at[offset],
            device_id={"grid": other},
            device_id_type=MESH,
        ).wait_recv()
    total = jnp.sum(sums[...], axis=0)[0:1, :]
    complementary_ref[...] = complementary_ref[...] / jnp.sqrt(total / (points * n) + 1e-06)
    for copy in copies:
        copy.wait_send()


def body(valence, conduction, potentials, eigenpotentials, valence_energy, conduction_energy):
    grid_rows = valence.shape[0]
    valence_count = valence.shape[1]
    conduction_count = conduction.shape[1]
    potential_count = potentials.shape[1]
    eigen_count = eigenpotentials.shape[1]
    n = lax.axis_size("grid")
    levels = n.bit_length() - 1
    points_total = grid_rows * n
    pair_count = potential_count * valence_count
    vmem = pl.BlockSpec(memory_space=pltpu.VMEM)

    joined = potentials.astype(jnp.float32)[:, :, None] * valence.astype(jnp.float32)[:, None, :]
    paired = joined.reshape(grid_rows, pair_count).astype(jnp.bfloat16)
    partial = contract_rows(paired, conduction)
    weight = (4.0 / points_total) / (valence_energy[:, None] - conduction_energy[None, :])

    plain = list(range(levels))
    crossed = [0, 2, 1] + plain[3:] if levels >= 3 else plain
    orders = [plain, crossed] * (conduction_count // 256)
    shape = (pair_count, conduction_count)
    scaled = pl.pallas_call(
        functools.partial(couple_kernel, n, orders),
        out_shape=jax.ShapeDtypeStruct(shape, jnp.bfloat16),
        in_specs=[vmem] * 2,
        out_specs=vmem,
        scratch_shapes=[
            pltpu.VMEM(shape, jnp.float32),
            pltpu.VMEM(shape, jnp.bfloat16),
            pltpu.VMEM(shape, jnp.bfloat16),
            pltpu.SemaphoreType.DMA((len(orders), 2 * levels)),
            pltpu.SemaphoreType.DMA((len(orders), 2 * levels)),
        ],
        compiler_params=pltpu.CompilerParams(
            collective_id=0, has_side_effects=True, vmem_limit_bytes=VMEM_BYTES
        ),
    )(partial, weight)

    combined = lax.dot_general(
        conduction, scaled, (((1,), (1,)), ((), ())), preferred_element_type=jnp.float32
    )
    response = jnp.sum(
        combined.reshape(grid_rows, potential_count, valence_count)
        * valence.astype(jnp.float32)[:, None, :],
        axis=2,
    )

    return pl.pallas_call(
        functools.partial(project_kernel, n),
        out_shape=(
            jax.ShapeDtypeStruct((eigen_count // n, potential_count), jnp.float32),
            jax.ShapeDtypeStruct((grid_rows, potential_count), jnp.float32),
        ),
        in_specs=[vmem] * 2,
        out_specs=(vmem, vmem),
        scratch_shapes=[
            pltpu.VMEM((eigen_count, potential_count), jnp.float32),
            pltpu.VMEM((eigen_count, potential_count), jnp.float32),
            pltpu.VMEM((eigen_count, potential_count), jnp.bfloat16),
            pltpu.VMEM((eigen_count, potential_count), jnp.bfloat16),
            pltpu.VMEM((n, 8, potential_count), jnp.float32),
            pltpu.SemaphoreType.DMA((2 * levels,)),
            pltpu.SemaphoreType.DMA((2 * levels,)),
            pltpu.SemaphoreType.DMA((n,)),
            pltpu.SemaphoreType.DMA((n,)),
        ],
        compiler_params=pltpu.CompilerParams(
            collective_id=1, has_side_effects=True, vmem_limit_bytes=VMEM_BYTES
        ),
    )(eigenpotentials, response)


def solution(mesh):
    return jax.shard_map(
        body,
        mesh=mesh,
        in_specs=(
            P(("grp", "grid"), None),
            P(("grp", "grid"), None),
            P(("grp", "grid"), None),
            P(("grp", "grid"), None),
            P("grp"),
            P("grp"),
        ),
        out_specs=(P(("grp", "grid"), None), P(("grp", "grid"), None)),
        check_vma=False,
    )
```

```python
import functools

import jax
import jax.numpy as jnp
from jax import lax
from jax.experimental import pallas as pl
from jax.experimental.pallas import tpu as pltpu
from jax.sharding import PartitionSpec as P

MESH = pl.DeviceIdType.MESH
VMEM_BYTES = 56 * 1024 * 1024


def contract_rows(left, right):
    return lax.dot_general(
        left, right, (((0,), (0,)), ((), ())), preferred_element_type=jnp.float32
    )


def bit_of(me, bit):
    return lax.rem(lax.div(me, 1 << bit), 2)


def partner_of(me, bit):
    return me + (1 - 2 * bit_of(me, bit)) * (1 << bit)


def aligned(row, step):
    return pl.multiple_of(row, step)


def couple_kernel(
    n, orders, pairs_ref, conduction_ref, valence_ref, weight_ref, response_ref,
    scaled, acc, sent, got, send_sem, recv_sem,
):
    levels = n.bit_length() - 1
    me = lax.axis_index("grid")
    rows, columns = scaled.shape
    unit = weight_ref.shape[0]
    block = rows // n
    width = columns // len(orders)

    barrier = pltpu.get_barrier_semaphore()
    for bit in range(levels):
        pl.semaphore_signal(
            barrier, inc=1, device_id={"grid": partner_of(me, bit)}, device_id_type=MESH
        )
    pl.semaphore_wait(barrier, levels)

    slots = [rows - (rows >> s) for s in range(levels)]
    bases = [[0] for _ in orders]
    copies = [[] for _ in orders]

    def start_halving(q, s):
        size = (n >> (s + 1)) * block
        cols = pl.ds(q * width, width)
        copy = pltpu.make_async_remote_copy(
            src_ref=sent.at[pl.ds(slots[s], size), cols],
            dst_ref=got.at[pl.ds(slots[s], size), cols],
            send_sem=send_sem.at[q, s],
            recv_sem=recv_sem.at[q, s],
            device_id={"grid": partner_of(me, orders[q][s])},
            device_id_type=MESH,
        )
        copy.start()
        copies[q].append(copy)

    strip = 2 * width
    tile = rows // 8
    first = bit_of(me, 0)
    leave, keep = (1 - first) * (rows // 2), first * (rows // 2)
    for h in range(columns // strip):
        strip_cols = pl.ds(h * strip, strip)

        def product(row, strip_cols=strip_cols):
            return jnp.dot(
                pairs_ref[pl.ds(aligned(row, tile), tile), :],
                conduction_ref[:, strip_cols],
                preferred_element_type=jnp.float32,
            )

        def send_tile(i, _, product=product, strip_cols=strip_cols):
            sent[pl.ds(aligned(i * tile, tile), tile), strip_cols] = product(
                leave + i * tile
            ).astype(jnp.bfloat16)
            return 0

        def keep_tile(i, _, product=product, strip_cols=strip_cols):
            acc[pl.ds(aligned(keep + i * tile, tile), tile), strip_cols] = product(keep + i * tile)
            return 0

        lax.fori_loop(0, 4, send_tile, 0)
        start_halving(2 * h, 0)
        start_halving(2 * h + 1, 0)
        lax.fori_loop(0, 4, keep_tile, 0)
    for q in range(len(orders)):
        bases[q].append(first * (n // 2))

    for s in range(1, levels + 1):
        for q, order in enumerate(orders):
            cols = pl.ds(q * width, width)
            base = bases[q][s]
            copies[q][s - 1].wait_recv()

            def term(row, offset, s=s, cols=cols):
                return acc[pl.ds(aligned(row + offset, unit), unit), cols] + got[
                    pl.ds(aligned(slots[s - 1] + offset, unit), unit), cols
                ].astype(jnp.float32)

            if s == levels:
                def finish(i, _, term=term, base=base, cols=cols):
                    value = term(base * block, i * unit) * weight_ref[:, cols]
                    scaled[pl.ds(aligned(base * block + i * unit, unit), unit), cols] = (
                        value.astype(jnp.bfloat16)
                    )
                    return 0

                lax.fori_loop(0, block // unit, finish, 0)
                continue
            half = n >> (s + 1)
            bit = bit_of(me, order[s])
            give, hold = (1 - bit) * half * block, bit * half * block

            def pack(i, _, term=term, base=base, give=give, s=s, cols=cols):
                sent[pl.ds(aligned(slots[s] + i * unit, unit), unit), cols] = term(
                    base * block, give + i * unit
                ).astype(jnp.bfloat16)
                return 0

            def add(i, _, term=term, base=base, hold=hold, cols=cols):
                acc[pl.ds(aligned(base * block + hold + i * unit, unit), unit), cols] = term(
                    base * block, hold + i * unit
                )
                return 0

            lax.fori_loop(0, half * block // unit, pack, 0)
            start_halving(q, s)
            lax.fori_loop(0, half * block // unit, add, 0)
            bases[q].append(base + bit * half)

    for s in reversed(range(levels)):
        for q, order in enumerate(orders):
            if s < levels - 1:
                copies[q][-1].wait_recv()
            size = (n >> (s + 1)) * block
            view = scaled.at[
                pl.ds(aligned(bases[q][s + 1] * block, unit), size), pl.ds(q * width, width)
            ]
            copy = pltpu.make_async_remote_copy(
                src_ref=view,
                dst_ref=view,
                send_sem=send_sem.at[q, 2 * levels - 1 - s],
                recv_sem=recv_sem.at[q, 2 * levels - 1 - s],
                device_id={"grid": partner_of(me, order[s])},
                device_id_type=MESH,
            )
            copy.start()
            copies[q].append(copy)

    group = 8

    def respond(row):
        combined = lax.dot_general(
            scaled[pl.ds(aligned(row * unit, group * unit), group * unit), :],
            conduction_ref[...],
            (((1,), (1,)), ((), ())),
            preferred_element_type=jnp.float32,
        )
        weighted = combined.reshape(group, unit, combined.shape[1]) * valence_ref[...][None]
        response_ref[pl.ds(aligned(row, group), group), :] = jnp.sum(weighted, axis=1)

    potentials = rows // unit
    for position, start in enumerate((first, 1 - first)):
        if position:
            for q in range(len(orders)):
                copies[q][-1].wait_recv()

        def step(i, _, start=start):
            respond(start * (potentials // 2) + i * group)
            return 0

        lax.fori_loop(0, potentials // 2 // group, step, 0)
    for q in range(len(orders)):
        for copy in copies[q]:
            copy.wait_send()


def phases_of(n):
    phases, weight = [], 1
    while weight < n:
        radix = min(4, n // weight)
        phases.append((weight, radix))
        weight *= radix
    return phases


def place_of(block, n):
    place, size = 0, n
    for weight, radix in phases_of(n):
        size //= radix
        place += (block // weight % radix) * size
    return place


def project_kernel(
    n, eigen_ref, response_ref, projected_ref, remainder_ref, total_ref,
    acc, got, gathered, low, sums, send_sem, recv_sem, sum_send, sum_recv,
):
    me = lax.axis_index("grid")
    points, eigens = eigen_ref.shape
    count = response_ref.shape[0]
    block = eigens // n
    packed = block // 2
    phases = phases_of(n)

    barrier = pltpu.get_barrier_semaphore()
    for offset in range(1, n):
        pl.semaphore_signal(
            barrier, inc=1, device_id={"grid": lax.rem(me + offset, n)}, device_id_type=MESH
        )

    response_low = response_ref[...].astype(jnp.bfloat16)
    strip = min(256, eigens)
    for start in range(0, eigens, strip):
        part = jnp.dot(
            response_low, eigen_ref[:, start:start + strip], preferred_element_type=jnp.float32
        ).T
        for b in range(strip // block):
            place = place_of(start // block + b, n) * packed
            for side in range(2):
                row = b * block + side * packed
                acc[place:place + packed, side * count:(side + 1) * count] = part[row:row + packed, :]
    pl.semaphore_wait(barrier, n - 1)

    def peer(weight, radix, digit, offset):
        other = lax.rem(digit + offset, radix)
        return other, me + (other - digit) * weight

    copies = []
    bases = [0]
    slot = 0
    size = n
    index = 0
    for weight, radix in phases:
        size //= radix
        height = size * packed
        digit = lax.rem(lax.div(me, weight), radix)
        arriving = []
        for offset in range(1, radix):
            other, device = peer(weight, radix, digit, offset)
            copy = pltpu.make_async_remote_copy(
                src_ref=acc.at[pl.ds(aligned((bases[-1] + other * size) * packed, packed), height)],
                dst_ref=got.at[pl.ds(slot, height)],
                send_sem=send_sem.at[index],
                recv_sem=recv_sem.at[index],
                device_id={"grid": device},
                device_id_type=MESH,
            )
            copy.start()
            arriving.append((copy, slot))
            slot += height
            index += 1
        bases.append(bases[-1] + digit * size)
        kept = pl.ds(aligned(bases[-1] * packed, packed), height)
        value = acc[kept, :]
        for copy, place in arriving:
            copy.wait_recv()
            value = value + got[place:place + height, :]
            copies.append(copy)
        acc[kept, :] = value

    own = acc[pl.ds(aligned(bases[-1] * packed, packed), packed), :]
    mine = jnp.concatenate([own[:, :count], own[:, count:]], axis=0)
    gathered[pl.ds(aligned(bases[-1] * block, block), block), :] = mine.astype(jnp.bfloat16)
    for level in reversed(range(len(phases))):
        weight, radix = phases[level]
        digit = lax.rem(lax.div(me, weight), radix)
        height = size * block
        view = gathered.at[pl.ds(aligned(bases[level + 1] * block, block), height)]
        arriving = []
        for offset in range(1, radix):
            _, device = peer(weight, radix, digit, offset)
            copy = pltpu.make_async_remote_copy(
                src_ref=view,
                dst_ref=view,
                send_sem=send_sem.at[index],
                recv_sem=recv_sem.at[index],
                device_id={"grid": device},
                device_id_type=MESH,
            )
            copy.start()
            copies.append(copy)
            other, device = peer(weight, radix, digit, radix - offset)
            place = gathered.at[pl.ds(aligned((bases[level] + other * size) * block, block), height)]
            arriving.append(pltpu.make_async_remote_copy(
                src_ref=place,
                dst_ref=place,
                send_sem=send_sem.at[index],
                recv_sem=recv_sem.at[index],
                device_id={"grid": device},
                device_id_type=MESH,
            ))
            index += 1
        for copy in arriving:
            copy.wait_recv()
        size *= radix
    for b in range(n):
        place = place_of(b, n) * block
        low[b * block:(b + 1) * block, :] = gathered[place:place + block, :]

    wide = low[...].astype(jnp.float32)
    remainder = response_ref[...] - lax.dot_general(
        wide.T.astype(jnp.bfloat16), eigen_ref[...], (((1,), (1,)), ((), ())),
        preferred_element_type=jnp.float32,
    )
    squared = remainder * remainder
    lanes = squared[:, :128]
    for start in range(128, points, 128):
        lanes = lanes + squared[:, start:start + 128]
    sums[me] = jnp.broadcast_to(
        jnp.sum(lanes.T, axis=0, keepdims=True), sums.shape[1:]
    )
    for offset in range(1, n):
        copy = pltpu.make_async_remote_copy(
            src_ref=sums.at[me],
            dst_ref=sums.at[me],
            send_sem=sum_send.at[offset],
            recv_sem=sum_recv.at[offset],
            device_id={"grid": lax.rem(me + offset, n)},
            device_id_type=MESH,
        )
        copy.start()
        copies.append(copy)
    remainder_ref[...] = remainder
    squares = jnp.sum(wide * wide, axis=0, keepdims=True)
    projected_ref[...] = mine / jnp.sqrt(squares / eigens + 1e-06)
    for offset in range(1, n):
        other = lax.rem(me + n - offset, n)
        pltpu.make_async_remote_copy(
            src_ref=sums.at[other],
            dst_ref=sums.at[other],
            send_sem=sum_send.at[offset],
            recv_sem=sum_recv.at[offset],
            device_id={"grid": other},
            device_id_type=MESH,
        ).wait_recv()
    total_ref[...] = jnp.sum(sums[...], axis=0)
    for copy in copies:
        copy.wait_send()


def body(valence, conduction, potentials, eigenpotentials, valence_energy, conduction_energy):
    grid_rows = valence.shape[0]
    valence_count = valence.shape[1]
    conduction_count = conduction.shape[1]
    potential_count = potentials.shape[1]
    eigen_count = eigenpotentials.shape[1]
    n = lax.axis_size("grid")
    levels = n.bit_length() - 1
    points_total = grid_rows * n
    pair_count = potential_count * valence_count
    vmem = pl.BlockSpec(memory_space=pltpu.VMEM)

    valence_wide = valence.T.astype(jnp.float32)
    joined = potentials.T.astype(jnp.float32)[:, None, :] * valence_wide[None, :, :]
    pairs = joined.reshape(pair_count, grid_rows).astype(jnp.bfloat16)
    weight = (4.0 / points_total) / (valence_energy[:, None] - conduction_energy[None, :])

    plain = list(range(levels))
    crossed = [0, 2, 1] + plain[3:] if levels >= 3 else plain
    orders = [plain, crossed] * (conduction_count // 256)
    shape = (pair_count, conduction_count)
    response = pl.pallas_call(
        functools.partial(couple_kernel, n, orders),
        out_shape=jax.ShapeDtypeStruct((potential_count, grid_rows), jnp.float32),
        in_specs=[vmem] * 4,
        out_specs=vmem,
        scratch_shapes=[
            pltpu.VMEM(shape, jnp.bfloat16),
            pltpu.VMEM(shape, jnp.float32),
            pltpu.VMEM(shape, jnp.bfloat16),
            pltpu.VMEM(shape, jnp.bfloat16),
            pltpu.SemaphoreType.DMA((len(orders), 2 * levels)),
            pltpu.SemaphoreType.DMA((len(orders), 2 * levels)),
        ],
        compiler_params=pltpu.CompilerParams(
            collective_id=0, has_side_effects=True, vmem_limit_bytes=VMEM_BYTES
        ),
    )(pairs, conduction, valence_wide, weight)

    transfers = 2 * sum(radix - 1 for _, radix in phases_of(n))
    projected, remainder, total = pl.pallas_call(
        functools.partial(project_kernel, n),
        out_shape=(
            jax.ShapeDtypeStruct((eigen_count // n, potential_count), jnp.float32),
            jax.ShapeDtypeStruct((potential_count, grid_rows), jnp.float32),
            jax.ShapeDtypeStruct((8, potential_count), jnp.float32),
        ),
        in_specs=[vmem] * 2,
        out_specs=(vmem, vmem, vmem),
        scratch_shapes=[
            pltpu.VMEM((eigen_count // 2, 2 * potential_count), jnp.float32),
            pltpu.VMEM((eigen_count // 2, 2 * potential_count), jnp.float32),
            pltpu.VMEM((eigen_count, potential_count), jnp.bfloat16),
            pltpu.VMEM((eigen_count, potential_count), jnp.bfloat16),
            pltpu.VMEM((n, 8, potential_count), jnp.float32),
            pltpu.SemaphoreType.DMA((transfers,)),
            pltpu.SemaphoreType.DMA((transfers,)),
            pltpu.SemaphoreType.DMA((n,)),
            pltpu.SemaphoreType.DMA((n,)),
        ],
        compiler_params=pltpu.CompilerParams(
            collective_id=1, has_side_effects=True, vmem_limit_bytes=VMEM_BYTES
        ),
    )(eigenpotentials, response)
    root = jnp.sqrt(total[0] / points_total + 1e-06)
    return projected, (remainder / root[:, None]).T


def solution(mesh):
    return jax.shard_map(
        body,
        mesh=mesh,
        in_specs=(
            P(("grp", "grid"), None),
            P(("grp", "grid"), None),
            P(("grp", "grid"), None),
            P(("grp", "grid"), None),
            P("grp"),
            P("grp"),
        ),
        out_specs=(P(("grp", "grid"), None), P(("grp", "grid"), None)),
        check_vma=False,
    )
```

```python
import functools

import jax
import jax.numpy as jnp
from jax import lax
from jax.experimental import pallas as pl
from jax.experimental.pallas import tpu as pltpu
from jax.sharding import PartitionSpec as P

MESH = pl.DeviceIdType.MESH
VMEM_BYTES = 56 * 1024 * 1024


def contract_rows(left, right):
    return lax.dot_general(
        left, right, (((0,), (0,)), ((), ())), preferred_element_type=jnp.float32
    )


def bit_of(me, bit):
    return lax.rem(lax.div(me, 1 << bit), 2)


def partner_of(me, bit):
    return me + (1 - 2 * bit_of(me, bit)) * (1 << bit)


def aligned(row, step):
    return pl.multiple_of(row, step)


def couple_kernel(
    n, orders, lags, valence_ref, conduction_ref, potential_ref, filled_ref, empty_ref, response_ref,
    wide, weight, scaled, acc, sent, got, send_sem, recv_sem,
):
    levels = n.bit_length() - 1
    me = lax.axis_index("grid")
    rows, columns = scaled.shape
    unit = valence_ref.shape[0]
    points = valence_ref.shape[1] * n
    block = rows // n
    width = columns // len(orders)

    barrier = pltpu.get_barrier_semaphore()
    for bit in range(levels):
        pl.semaphore_signal(
            barrier, inc=1, device_id={"grid": partner_of(me, bit)}, device_id_type=MESH
        )
    wide[...] = valence_ref[...].astype(jnp.float32)
    energies = jnp.broadcast_to(filled_ref[...], (8, unit)).T[:, 0:1]
    weight[...] = (4.0 / points) / (energies - empty_ref[...])

    slots = [rows - (rows >> s) for s in range(levels)]
    bases = [[0] for _ in orders]
    copies = [[] for _ in orders]

    def start_halving(q, s):
        size = (n >> (s + 1)) * block
        cols = pl.ds(q * width, width)
        copy = pltpu.make_async_remote_copy(
            src_ref=sent.at[pl.ds(slots[s], size), cols],
            dst_ref=got.at[pl.ds(slots[s], size), cols],
            send_sem=send_sem.at[q, s],
            recv_sem=recv_sem.at[q, s],
            device_id={"grid": partner_of(me, orders[q][s])},
            device_id_type=MESH,
        )
        copy.start()
        copies[q].append(copy)

    group = 8
    tile = group * unit
    tiles = rows // tile // 2
    first = bit_of(me, 0)

    def product(index):
        potential = potential_ref[pl.ds(aligned(index * group, group), group), :]
        pairs = potential[:, None, :] * wide[...][None]
        return jnp.dot(
            pairs.reshape(tile, wide.shape[1]).astype(jnp.bfloat16),
            conduction_ref[...],
            preferred_element_type=jnp.float32,
        )

    def send_tile(i, _):
        sent[pl.ds(aligned(i * tile, tile), tile), :] = product(
            (1 - first) * tiles + i
        ).astype(jnp.bfloat16)
        return 0

    def keep_tile(i, _):
        index = first * tiles + i
        acc[pl.ds(aligned(index * tile, tile), tile), :] = product(index)
        return 0

    lax.fori_loop(0, tiles, send_tile, 0)
    pl.semaphore_wait(barrier, levels)
    for q in range(len(orders)):
        start_halving(q, 0)
    lax.fori_loop(0, tiles, keep_tile, 0)
    for q in range(len(orders)):
        bases[q].append(first * (n // 2))

    def halve(q, s):
        order = orders[q]
        cols = pl.ds(q * width, width)
        base = bases[q][s]
        copies[q][s - 1].wait_recv()

        def term(row, offset):
            return acc[pl.ds(aligned(row + offset, unit), unit), cols] + got[
                pl.ds(aligned(slots[s - 1] + offset, unit), unit), cols
            ].astype(jnp.float32)

        if s == levels:
            def finish(i, _):
                value = term(base * block, i * unit) * weight[:, cols]
                scaled[pl.ds(aligned(base * block + i * unit, unit), unit), cols] = (
                    value.astype(jnp.bfloat16)
                )
                return 0

            lax.fori_loop(0, block // unit, finish, 0)
            return
        half = n >> (s + 1)
        bit = bit_of(me, order[s])
        give, hold = (1 - bit) * half * block, bit * half * block

        def pack(i, _):
            sent[pl.ds(aligned(slots[s] + i * unit, unit), unit), cols] = term(
                base * block, give + i * unit
            ).astype(jnp.bfloat16)
            return 0

        def add(i, _):
            acc[pl.ds(aligned(base * block + hold + i * unit, unit), unit), cols] = term(
                base * block, hold + i * unit
            )
            return 0

        lax.fori_loop(0, half * block // unit, pack, 0)
        start_halving(q, s)
        lax.fori_loop(0, half * block // unit, add, 0)
        bases[q].append(base + bit * half)

    def double(q, s):
        if s < levels - 1:
            copies[q][-1].wait_recv()
        size = (n >> (s + 1)) * block
        view = scaled.at[
            pl.ds(aligned(bases[q][s + 1] * block, unit), size), pl.ds(q * width, width)
        ]
        copy = pltpu.make_async_remote_copy(
            src_ref=view,
            dst_ref=view,
            send_sem=send_sem.at[q, 2 * levels - 1 - s],
            recv_sem=recv_sem.at[q, 2 * levels - 1 - s],
            device_id={"grid": partner_of(me, orders[q][s])},
            device_id_type=MESH,
        )
        copy.start()
        copies[q].append(copy)

    events = sorted(
        (event + lags[q], q, event) for q in range(len(orders)) for event in range(1, 2 * levels)
    )
    for _, q, event in events:
        if event <= levels:
            halve(q, event)
        if event >= levels:
            double(q, 2 * levels - 1 - event)

    def respond(row):
        combined = lax.dot_general(
            scaled[pl.ds(aligned(row * unit, group * unit), group * unit), :],
            conduction_ref[...],
            (((1,), (1,)), ((), ())),
            preferred_element_type=jnp.float32,
        )
        weighted = combined.reshape(group, unit, combined.shape[1]) * wide[...][None]
        response_ref[pl.ds(aligned(row, group), group), :] = jnp.sum(weighted, axis=1)

    potentials = rows // unit
    for position, start in enumerate((first, 1 - first)):
        if position:
            for q in range(len(orders)):
                copies[q][-1].wait_recv()

        def step(i, _, start=start):
            respond(start * (potentials // 2) + i * group)
            return 0

        lax.fori_loop(0, potentials // 2 // group, step, 0)
    for q in range(len(orders)):
        for copy in copies[q]:
            copy.wait_send()


def phases_of(n):
    phases, weight = [], 1
    while weight < n:
        radix = min(4, n // weight)
        phases.append((weight, radix))
        weight *= radix
    return phases


def place_of(block, n):
    place, size = 0, n
    for weight, radix in phases_of(n):
        size //= radix
        place += (block // weight % radix) * size
    return place


def project_kernel(
    n, eigen_ref, response_ref, projected_ref, remainder_ref, total_ref,
    acc, got, gathered, low, sums, send_sem, recv_sem, sum_send, sum_recv,
):
    me = lax.axis_index("grid")
    points, eigens = eigen_ref.shape
    count = response_ref.shape[0]
    block = eigens // n
    packed = block // 2
    low_rows = gathered.shape[0] // n
    phases = phases_of(n)

    barrier = pltpu.get_barrier_semaphore()
    for offset in range(1, n):
        pl.semaphore_signal(
            barrier, inc=1, device_id={"grid": lax.rem(me + offset, n)}, device_id_type=MESH
        )

    response_low = response_ref[...].astype(jnp.bfloat16)
    strip = min(256, eigens)
    for start in range(0, eigens, strip):
        part = jnp.dot(
            response_low, eigen_ref[:, start:start + strip], preferred_element_type=jnp.float32
        ).T
        for b in range(strip // block):
            place = place_of(start // block + b, n) * packed
            for side in range(2):
                row = b * block + side * packed
                acc[place:place + packed, side * count:(side + 1) * count] = part[row:row + packed, :]
    pl.semaphore_wait(barrier, n - 1)

    def peer(weight, radix, digit, offset):
        other = lax.rem(digit + offset, radix)
        return other, me + (other - digit) * weight

    copies = []
    bases = [0]
    slot = 0
    size = n
    index = 0
    for weight, radix in phases:
        size //= radix
        height = size * packed
        digit = lax.rem(lax.div(me, weight), radix)
        arriving = []
        for offset in range(1, radix):
            other, device = peer(weight, radix, digit, offset)
            copy = pltpu.make_async_remote_copy(
                src_ref=acc.at[pl.ds(aligned((bases[-1] + other * size) * packed, packed), height)],
                dst_ref=got.at[pl.ds(slot, height)],
                send_sem=send_sem.at[index],
                recv_sem=recv_sem.at[index],
                device_id={"grid": device},
                device_id_type=MESH,
            )
            copy.start()
            arriving.append((copy, slot))
            slot += height
            index += 1
        bases.append(bases[-1] + digit * size)
        kept = pl.ds(aligned(bases[-1] * packed, packed), height)
        value = acc[kept, :]
        for copy, place in arriving:
            copy.wait_recv()
            value = value + got[place:place + height, :]
            copies.append(copy)
        acc[kept, :] = value

    own = acc[pl.ds(aligned(bases[-1] * packed, packed), packed), :]
    mine = jnp.concatenate([own[:, :count], own[:, count:]], axis=0)
    gathered[pl.ds(aligned(bases[-1] * low_rows, low_rows), low_rows), :] = (
        own if low_rows == packed else mine
    ).astype(jnp.bfloat16)
    for level in reversed(range(len(phases))):
        weight, radix = phases[level]
        digit = lax.rem(lax.div(me, weight), radix)
        height = size * low_rows
        view = gathered.at[pl.ds(aligned(bases[level + 1] * low_rows, low_rows), height)]
        arriving = []
        for offset in range(1, radix):
            _, device = peer(weight, radix, digit, offset)
            copy = pltpu.make_async_remote_copy(
                src_ref=view,
                dst_ref=view,
                send_sem=send_sem.at[index],
                recv_sem=recv_sem.at[index],
                device_id={"grid": device},
                device_id_type=MESH,
            )
            copy.start()
            copies.append(copy)
            other, device = peer(weight, radix, digit, radix - offset)
            place = gathered.at[
                pl.ds(aligned((bases[level] + other * size) * low_rows, low_rows), height)
            ]
            arriving.append(pltpu.make_async_remote_copy(
                src_ref=place,
                dst_ref=place,
                send_sem=send_sem.at[index],
                recv_sem=recv_sem.at[index],
                device_id={"grid": device},
                device_id_type=MESH,
            ))
            index += 1
        for copy in arriving:
            copy.wait_recv()
        size *= radix
    for b in range(n):
        place = place_of(b, n) * low_rows
        for part in range(block // low_rows):
            row = b * block + part * low_rows
            low[row:row + low_rows, :] = gathered[
                place:place + low_rows, part * count:(part + 1) * count
            ]

    wide = low[...].astype(jnp.float32)
    remainder = response_ref[...] - lax.dot_general(
        wide.T.astype(jnp.bfloat16), eigen_ref[...], (((1,), (1,)), ((), ())),
        preferred_element_type=jnp.float32,
    )
    squared = remainder * remainder
    lanes = squared[:, :128]
    for start in range(128, points, 128):
        lanes = lanes + squared[:, start:start + 128]
    sums[me] = jnp.broadcast_to(
        jnp.sum(lanes.T, axis=0, keepdims=True), sums.shape[1:]
    )
    for offset in range(1, n):
        copy = pltpu.make_async_remote_copy(
            src_ref=sums.at[me],
            dst_ref=sums.at[me],
            send_sem=sum_send.at[offset],
            recv_sem=sum_recv.at[offset],
            device_id={"grid": lax.rem(me + offset, n)},
            device_id_type=MESH,
        )
        copy.start()
        copies.append(copy)
    remainder_ref[...] = remainder
    squares = jnp.sum(wide * wide, axis=0, keepdims=True)
    projected_ref[...] = mine / jnp.sqrt(squares / eigens + 1e-06)
    for offset in range(1, n):
        other = lax.rem(me + n - offset, n)
        pltpu.make_async_remote_copy(
            src_ref=sums.at[other],
            dst_ref=sums.at[other],
            send_sem=sum_send.at[offset],
            recv_sem=sum_recv.at[offset],
            device_id={"grid": other},
            device_id_type=MESH,
        ).wait_recv()
    total_ref[...] = jnp.sum(sums[...], axis=0)
    for copy in copies:
        copy.wait_send()


def body(valence, conduction, potentials, eigenpotentials, valence_energy, conduction_energy):
    grid_rows = valence.shape[0]
    valence_count = valence.shape[1]
    conduction_count = conduction.shape[1]
    potential_count = potentials.shape[1]
    eigen_count = eigenpotentials.shape[1]
    n = lax.axis_size("grid")
    levels = n.bit_length() - 1
    points_total = grid_rows * n
    pair_count = potential_count * valence_count
    vmem = pl.BlockSpec(memory_space=pltpu.VMEM)

    plain = list(range(levels))
    crossed = [0, 2, 1] + plain[3:] if levels >= 3 else plain
    chunks = conduction_count // 128
    orders = [crossed if q % 4 == 3 else plain for q in range(chunks)]
    lags = [1 if q % 4 == 1 else 0 for q in range(chunks)]
    shape = (pair_count, conduction_count)
    response = pl.pallas_call(
        functools.partial(couple_kernel, n, orders, lags),
        out_shape=jax.ShapeDtypeStruct((potential_count, grid_rows), jnp.float32),
        in_specs=[vmem] * 5,
        out_specs=vmem,
        scratch_shapes=[
            pltpu.VMEM((valence_count, grid_rows), jnp.float32),
            pltpu.VMEM((valence_count, conduction_count), jnp.float32),
            pltpu.VMEM(shape, jnp.bfloat16),
            pltpu.VMEM(shape, jnp.float32),
            pltpu.VMEM(shape, jnp.bfloat16),
            pltpu.VMEM(shape, jnp.bfloat16),
            pltpu.SemaphoreType.DMA((len(orders), 2 * levels)),
            pltpu.SemaphoreType.DMA((len(orders), 2 * levels)),
        ],
        compiler_params=pltpu.CompilerParams(
            collective_id=0, has_side_effects=True, vmem_limit_bytes=VMEM_BYTES
        ),
    )(
        valence.T, conduction, potentials.T.astype(jnp.float32),
        valence_energy[None, :], conduction_energy[None, :],
    )

    fold = 2 if eigen_count // n % 32 == 0 else 1
    transfers = 2 * sum(radix - 1 for _, radix in phases_of(n))
    projected, remainder, total = pl.pallas_call(
        functools.partial(project_kernel, n),
        out_shape=(
            jax.ShapeDtypeStruct((eigen_count // n, potential_count), jnp.float32),
            jax.ShapeDtypeStruct((potential_count, grid_rows), jnp.float32),
            jax.ShapeDtypeStruct((8, potential_count), jnp.float32),
        ),
        in_specs=[vmem] * 2,
        out_specs=(vmem, vmem, vmem),
        scratch_shapes=[
            pltpu.VMEM((eigen_count // 2, 2 * potential_count), jnp.float32),
            pltpu.VMEM((eigen_count // 2, 2 * potential_count), jnp.float32),
            pltpu.VMEM((eigen_count // fold, fold * potential_count), jnp.bfloat16),
            pltpu.VMEM((eigen_count, potential_count), jnp.bfloat16),
            pltpu.VMEM((n, 8, potential_count), jnp.float32),
            pltpu.SemaphoreType.DMA((transfers,)),
            pltpu.SemaphoreType.DMA((transfers,)),
            pltpu.SemaphoreType.DMA((n,)),
            pltpu.SemaphoreType.DMA((n,)),
        ],
        compiler_params=pltpu.CompilerParams(
            collective_id=1, has_side_effects=True, vmem_limit_bytes=VMEM_BYTES
        ),
    )(eigenpotentials, response)
    root = jnp.sqrt(total[0] / points_total + 1e-06)
    return projected, (remainder / root[:, None]).T


def solution(mesh):
    return jax.shard_map(
        body,
        mesh=mesh,
        in_specs=(
            P(("grp", "grid"), None),
            P(("grp", "grid"), None),
            P(("grp", "grid"), None),
            P(("grp", "grid"), None),
            P("grp"),
            P("grp"),
        ),
        out_specs=(P(("grp", "grid"), None), P(("grp", "grid"), None)),
        check_vma=False,
    )
```

```python
import functools

import jax
import jax.numpy as jnp
from jax import lax
from jax.experimental import pallas as pl
from jax.experimental.pallas import tpu as pltpu
from jax.sharding import PartitionSpec as P

MESH = pl.DeviceIdType.MESH
VMEM_BYTES = 56 * 1024 * 1024


def contract_rows(left, right):
    return lax.dot_general(
        left, right, (((0,), (0,)), ((), ())), preferred_element_type=jnp.float32
    )


def bit_of(me, bit):
    return lax.rem(lax.div(me, 1 << bit), 2)


def partner_of(me, bit):
    return me + (1 - 2 * bit_of(me, bit)) * (1 << bit)


def aligned(row, step):
    return pl.multiple_of(row, step)


def couple_kernel(
    n, orders, lags, valence_ref, conduction_ref, potential_ref, filled_ref, empty_ref, response_ref,
    wide, factor, weight, scaled, acc, sent, got, send_sem, recv_sem,
):
    levels = n.bit_length() - 1
    me = lax.axis_index("grid")
    rows, columns = scaled.shape
    unit = valence_ref.shape[0]
    points = valence_ref.shape[1] * n
    block = rows // n
    width = columns // len(orders)

    barrier = pltpu.get_barrier_semaphore()
    for bit in range(levels):
        pl.semaphore_signal(
            barrier, inc=1, device_id={"grid": partner_of(me, bit)}, device_id_type=MESH
        )
    wide[...] = valence_ref[...].astype(jnp.float32)
    factor[...] = potential_ref[...].astype(jnp.float32)
    energies = jnp.broadcast_to(filled_ref[...], (8, unit)).T[:, 0:1]
    weight[...] = (4.0 / points) / (energies - empty_ref[...])

    slots = [rows - (rows >> s) for s in range(levels)]
    bases = [[0] for _ in orders]
    copies = [[] for _ in orders]

    def start_halving(q, s):
        size = (n >> (s + 1)) * block
        cols = pl.ds(q * width, width)
        copy = pltpu.make_async_remote_copy(
            src_ref=sent.at[pl.ds(slots[s], size), cols],
            dst_ref=got.at[pl.ds(slots[s], size), cols],
            send_sem=send_sem.at[q, s],
            recv_sem=recv_sem.at[q, s],
            device_id={"grid": partner_of(me, orders[q][s])},
            device_id_type=MESH,
        )
        copy.start()
        copies[q].append(copy)

    group = 8
    tile = group * unit
    tiles = rows // tile // 2
    first = bit_of(me, 0)

    def product(index):
        potential = factor[pl.ds(aligned(index * group, group), group), :]
        pairs = potential[:, None, :] * wide[...][None]
        return jnp.dot(
            pairs.reshape(tile, wide.shape[1]).astype(jnp.bfloat16),
            conduction_ref[...],
            preferred_element_type=jnp.float32,
        )

    def send_tile(i, _):
        sent[pl.ds(aligned(i * tile, tile), tile), :] = product(
            (1 - first) * tiles + i
        ).astype(jnp.bfloat16)
        return 0

    def keep_tile(i, _):
        index = first * tiles + i
        acc[pl.ds(aligned(index * tile, tile), tile), :] = product(index)
        return 0

    lax.fori_loop(0, tiles, send_tile, 0)
    pl.semaphore_wait(barrier, levels)
    for q in range(len(orders)):
        start_halving(q, 0)
    lax.fori_loop(0, tiles, keep_tile, 0)
    for q in range(len(orders)):
        bases[q].append(first * (n // 2))

    def halve(q, s):
        order = orders[q]
        cols = pl.ds(q * width, width)
        base = bases[q][s]
        copies[q][s - 1].wait_recv()

        def term(row, offset):
            return acc[pl.ds(aligned(row + offset, unit), unit), cols] + got[
                pl.ds(aligned(slots[s - 1] + offset, unit), unit), cols
            ].astype(jnp.float32)

        if s == levels:
            def finish(i, _):
                value = term(base * block, i * unit) * weight[:, cols]
                scaled[pl.ds(aligned(base * block + i * unit, unit), unit), cols] = (
                    value.astype(jnp.bfloat16)
                )
                return 0

            lax.fori_loop(0, block // unit, finish, 0)
            return
        half = n >> (s + 1)
        bit = bit_of(me, order[s])
        give, hold = (1 - bit) * half * block, bit * half * block

        def pack(i, _):
            sent[pl.ds(aligned(slots[s] + i * unit, unit), unit), cols] = term(
                base * block, give + i * unit
            ).astype(jnp.bfloat16)
            return 0

        def add(i, _):
            acc[pl.ds(aligned(base * block + hold + i * unit, unit), unit), cols] = term(
                base * block, hold + i * unit
            )
            return 0

        lax.fori_loop(0, half * block // unit, pack, 0)
        start_halving(q, s)
        lax.fori_loop(0, half * block // unit, add, 0)
        bases[q].append(base + bit * half)

    def double(q, s):
        if s < levels - 1:
            copies[q][-1].wait_recv()
        size = (n >> (s + 1)) * block
        view = scaled.at[
            pl.ds(aligned(bases[q][s + 1] * block, unit), size), pl.ds(q * width, width)
        ]
        copy = pltpu.make_async_remote_copy(
            src_ref=view,
            dst_ref=view,
            send_sem=send_sem.at[q, 2 * levels - 1 - s],
            recv_sem=recv_sem.at[q, 2 * levels - 1 - s],
            device_id={"grid": partner_of(me, orders[q][s])},
            device_id_type=MESH,
        )
        copy.start()
        copies[q].append(copy)

    events = sorted(
        (event + lags[q], q, event) for q in range(len(orders)) for event in range(1, 2 * levels)
    )
    for _, q, event in events:
        if event <= levels:
            halve(q, event)
        if event >= levels:
            double(q, 2 * levels - 1 - event)

    def respond(row):
        combined = lax.dot_general(
            scaled[pl.ds(aligned(row * unit, group * unit), group * unit), :],
            conduction_ref[...],
            (((1,), (1,)), ((), ())),
            preferred_element_type=jnp.float32,
        )
        weighted = combined.reshape(group, unit, combined.shape[1]) * wide[...][None]
        response_ref[pl.ds(aligned(row, group), group), :] = jnp.sum(weighted, axis=1)

    potentials = rows // unit
    for position, start in enumerate((first, 1 - first)):
        if position:
            for q in range(len(orders)):
                copies[q][-1].wait_recv()

        def step(i, _, start=start):
            respond(start * (potentials // 2) + i * group)
            return 0

        lax.fori_loop(0, potentials // 2 // group, step, 0)
    for q in range(len(orders)):
        for copy in copies[q]:
            copy.wait_send()


def phases_of(n):
    phases, weight = [], 1
    while weight < n:
        radix = min(4, n // weight)
        phases.append((weight, radix))
        weight *= radix
    return phases


def place_of(block, n):
    place, size = 0, n
    for weight, radix in phases_of(n):
        size //= radix
        place += (block // weight % radix) * size
    return place


def project_kernel(
    n, eigen_ref, response_ref, projected_ref, complementary_ref,
    acc, got, gathered, low, sums, send_sem, recv_sem, sum_send, sum_recv,
):
    me = lax.axis_index("grid")
    points, eigens = eigen_ref.shape
    count = response_ref.shape[0]
    block = eigens // n
    packed = block // 2
    low_rows = gathered.shape[0] // n
    phases = phases_of(n)

    barrier = pltpu.get_barrier_semaphore()
    for offset in range(1, n):
        pl.semaphore_signal(
            barrier, inc=1, device_id={"grid": lax.rem(me + offset, n)}, device_id_type=MESH
        )

    response_low = response_ref[...].astype(jnp.bfloat16)
    strip = min(256, eigens)
    for start in range(0, eigens, strip):
        part = jnp.dot(
            response_low, eigen_ref[:, start:start + strip], preferred_element_type=jnp.float32
        ).T
        for b in range(strip // block):
            place = place_of(start // block + b, n) * packed
            for side in range(2):
                row = b * block + side * packed
                acc[place:place + packed, side * count:(side + 1) * count] = part[row:row + packed, :]
    pl.semaphore_wait(barrier, n - 1)

    def peer(weight, radix, digit, offset):
        other = lax.rem(digit + offset, radix)
        return other, me + (other - digit) * weight

    copies = []
    bases = [0]
    slot = 0
    size = n
    index = 0
    for weight, radix in phases:
        size //= radix
        height = size * packed
        digit = lax.rem(lax.div(me, weight), radix)
        arriving = []
        for offset in range(1, radix):
            other, device = peer(weight, radix, digit, offset)
            copy = pltpu.make_async_remote_copy(
                src_ref=acc.at[pl.ds(aligned((bases[-1] + other * size) * packed, packed), height)],
                dst_ref=got.at[pl.ds(slot, height)],
                send_sem=send_sem.at[index],
                recv_sem=recv_sem.at[index],
                device_id={"grid": device},
                device_id_type=MESH,
            )
            copy.start()
            arriving.append((copy, slot))
            slot += height
            index += 1
        bases.append(bases[-1] + digit * size)
        kept = pl.ds(aligned(bases[-1] * packed, packed), height)
        value = acc[kept, :]
        for copy, place in arriving:
            copy.wait_recv()
            value = value + got[place:place + height, :]
            copies.append(copy)
        acc[kept, :] = value

    own = acc[pl.ds(aligned(bases[-1] * packed, packed), packed), :]
    mine = jnp.concatenate([own[:, :count], own[:, count:]], axis=0)
    gathered[pl.ds(aligned(bases[-1] * low_rows, low_rows), low_rows), :] = (
        own if low_rows == packed else mine
    ).astype(jnp.bfloat16)
    for level in reversed(range(len(phases))):
        weight, radix = phases[level]
        digit = lax.rem(lax.div(me, weight), radix)
        height = size * low_rows
        view = gathered.at[pl.ds(aligned(bases[level + 1] * low_rows, low_rows), height)]
        arriving = []
        for offset in range(1, radix):
            _, device = peer(weight, radix, digit, offset)
            copy = pltpu.make_async_remote_copy(
                src_ref=view,
                dst_ref=view,
                send_sem=send_sem.at[index],
                recv_sem=recv_sem.at[index],
                device_id={"grid": device},
                device_id_type=MESH,
            )
            copy.start()
            copies.append(copy)
            other, device = peer(weight, radix, digit, radix - offset)
            place = gathered.at[
                pl.ds(aligned((bases[level] + other * size) * low_rows, low_rows), height)
            ]
            arriving.append(pltpu.make_async_remote_copy(
                src_ref=place,
                dst_ref=place,
                send_sem=send_sem.at[index],
                recv_sem=recv_sem.at[index],
                device_id={"grid": device},
                device_id_type=MESH,
            ))
            index += 1
        for copy in arriving:
            copy.wait_recv()
        size *= radix
    for b in range(n):
        place = place_of(b, n) * low_rows
        for part in range(block // low_rows):
            row = b * block + part * low_rows
            low[row:row + low_rows, :] = gathered[
                place:place + low_rows, part * count:(part + 1) * count
            ]

    wide = low[...].astype(jnp.float32)
    remainder = response_ref[...] - lax.dot_general(
        wide.T.astype(jnp.bfloat16), eigen_ref[...], (((1,), (1,)), ((), ())),
        preferred_element_type=jnp.float32,
    )
    squared = remainder * remainder
    lanes = squared[:, :128]
    for start in range(128, points, 128):
        lanes = lanes + squared[:, start:start + 128]
    sums[me] = jnp.broadcast_to(
        jnp.sum(lanes.T, axis=0, keepdims=True), sums.shape[1:]
    )
    for offset in range(1, n):
        copy = pltpu.make_async_remote_copy(
            src_ref=sums.at[me],
            dst_ref=sums.at[me],
            send_sem=sum_send.at[offset],
            recv_sem=sum_recv.at[offset],
            device_id={"grid": lax.rem(me + offset, n)},
            device_id_type=MESH,
        )
        copy.start()
        copies.append(copy)
    complementary_ref[...] = remainder
    squares = jnp.sum(wide * wide, axis=0, keepdims=True)
    projected_ref[...] = mine / jnp.sqrt(squares / eigens + 1e-06)
    for offset in range(1, n):
        other = lax.rem(me + n - offset, n)
        pltpu.make_async_remote_copy(
            src_ref=sums.at[other],
            dst_ref=sums.at[other],
            send_sem=sum_send.at[offset],
            recv_sem=sum_recv.at[offset],
            device_id={"grid": other},
            device_id_type=MESH,
        ).wait_recv()
    total = jnp.sum(sums[...], axis=0).T[:, 0:1]
    complementary_ref[...] = complementary_ref[...] / jnp.sqrt(total / (points * n) + 1e-06)
    for copy in copies:
        copy.wait_send()


def body(valence, conduction, potentials, eigenpotentials, valence_energy, conduction_energy):
    grid_rows = valence.shape[0]
    valence_count = valence.shape[1]
    conduction_count = conduction.shape[1]
    potential_count = potentials.shape[1]
    eigen_count = eigenpotentials.shape[1]
    n = lax.axis_size("grid")
    levels = n.bit_length() - 1
    points_total = grid_rows * n
    pair_count = potential_count * valence_count
    vmem = pl.BlockSpec(memory_space=pltpu.VMEM)

    plain = list(range(levels))
    crossed = [0, 2, 1] + plain[3:] if levels >= 3 else plain
    chunks = conduction_count // 128
    orders = [crossed if q % 2 == 1 else plain for q in range(chunks)]
    lags = [(0, 0, 1, 1)[q % 4] for q in range(chunks)]
    shape = (pair_count, conduction_count)
    response = pl.pallas_call(
        functools.partial(couple_kernel, n, orders, lags),
        out_shape=jax.ShapeDtypeStruct((potential_count, grid_rows), jnp.float32),
        in_specs=[vmem] * 5,
        out_specs=vmem,
        scratch_shapes=[
            pltpu.VMEM((valence_count, grid_rows), jnp.float32),
            pltpu.VMEM((potential_count, grid_rows), jnp.float32),
            pltpu.VMEM((valence_count, conduction_count), jnp.float32),
            pltpu.VMEM(shape, jnp.bfloat16),
            pltpu.VMEM(shape, jnp.float32),
            pltpu.VMEM(shape, jnp.bfloat16),
            pltpu.VMEM(shape, jnp.bfloat16),
            pltpu.SemaphoreType.DMA((len(orders), 2 * levels)),
            pltpu.SemaphoreType.DMA((len(orders), 2 * levels)),
        ],
        compiler_params=pltpu.CompilerParams(
            collective_id=0, has_side_effects=True, vmem_limit_bytes=VMEM_BYTES
        ),
    )(
        valence.T, conduction, potentials.T,
        valence_energy[None, :], conduction_energy[None, :],
    )

    fold = 2 if eigen_count // n % 32 == 0 else 1
    transfers = 2 * sum(radix - 1 for _, radix in phases_of(n))
    projected, complementary = pl.pallas_call(
        functools.partial(project_kernel, n),
        out_shape=(
            jax.ShapeDtypeStruct((eigen_count // n, potential_count), jnp.float32),
            jax.ShapeDtypeStruct((potential_count, grid_rows), jnp.float32),
        ),
        in_specs=[vmem] * 2,
        out_specs=(vmem, vmem),
        scratch_shapes=[
            pltpu.VMEM((eigen_count // 2, 2 * potential_count), jnp.float32),
            pltpu.VMEM((eigen_count // 2, 2 * potential_count), jnp.float32),
            pltpu.VMEM((eigen_count // fold, fold * potential_count), jnp.bfloat16),
            pltpu.VMEM((eigen_count, potential_count), jnp.bfloat16),
            pltpu.VMEM((n, 8, potential_count), jnp.float32),
            pltpu.SemaphoreType.DMA((transfers,)),
            pltpu.SemaphoreType.DMA((transfers,)),
            pltpu.SemaphoreType.DMA((n,)),
            pltpu.SemaphoreType.DMA((n,)),
        ],
        compiler_params=pltpu.CompilerParams(
            collective_id=1, has_side_effects=True, vmem_limit_bytes=VMEM_BYTES
        ),
    )(eigenpotentials, response)
    return projected, complementary.T


def solution(mesh):
    return jax.shard_map(
        body,
        mesh=mesh,
        in_specs=(
            P(("grp", "grid"), None),
            P(("grp", "grid"), None),
            P(("grp", "grid"), None),
            P(("grp", "grid"), None),
            P("grp"),
            P("grp"),
        ),
        out_specs=(P(("grp", "grid"), None), P(("grp", "grid"), None)),
        check_vma=False,
    )
```
